256 devices in a mesh: tm: 32 (over y_lo, z, core), stn: 8 (over x, y_hi).
Axes of the slice: x: 4, y: 4 (y_hi: 2, y_lo: 2; y = y_hi * 2 + y_lo), z: 8, core: 2. Of those that a mesh axis runs over, the one named last changes fastest.
Arguments:
- voltages: bfloat16 [1024, 262144], P('stn', 'tm'), may hold values from -12 to 12, as said below
- fir_taps: float32 [12, 512], replicated, may hold values from -0.02 to 0.02
Outputs:
- visibilities: float32 [256, 2, 1024, 1024], P('tm', None, 'stn')
The draws below stay inside these ranges and needn't reach their ends.
Inputs may be any that keep to these rules, and one draw needn't show every extreme that they name: `voltages`: whole numbers. Each input holds a common sky signal, delayed by up to 64 samples, plus its own noise.
All inputs are finite; a program needn't handle non-finite values.
Results may differ from the reference program's by a relative error of at most 0.0022.
Values may be sent and summed in bfloat16 or wider, within the bound.
A program may use at most 128 MiB of HBM per device.

```python
import jax
import jax.numpy as jnp
from jax import lax

INPUTS = 1024
FRAME = 512
NCH = 256
TAPS = 12
FRAMES = 512
SAMPLES = 262144
DELAY = 64
N_STN = 8


def draw_voltages(key, part):
    key = jax.random.fold_in(key, 7)
    sky_key, noise_key, delay_key = jax.random.split(key, 3)
    sky_signal = jax.random.randint(sky_key, (SAMPLES + DELAY,), -6, 7)
    delays = jax.random.randint(delay_key, (INPUTS,), 0, DELAY + 1)
    noise_part = jax.random.randint(noise_key, (INPUTS, SAMPLES), -6, 7)
    shifted = jax.vmap(lambda delay_one: lax.dynamic_slice(sky_signal, (delay_one,), (SAMPLES,)))(delays)
    return (shifted + noise_part).astype(jnp.float32).astype(jnp.bfloat16)


def gaussian(rng, dims, width, most, dtype=jnp.bfloat16):
    return jnp.clip(width * jax.random.normal(rng, dims, jnp.float32), -most, most).astype(dtype)


def setup_inputs(seed: int = 0) -> dict:
    seeds = jax.random.split(jax.random.key(seed), 3)
    voltages = draw_voltages(jax.random.fold_in(seeds[2], 71), 0)
    fir_taps = gaussian(seeds[1], (TAPS, FRAME), 0.0034, 0.02, jnp.float32)
    return dict(voltages=voltages, fir_taps=fir_taps)


def channelise(input_block, fir_taps):
    sample_field = input_block.astype(jnp.float32)
    leading = jnp.zeros((sample_field.shape[0], TAPS - 1, FRAME), jnp.float32)
    padded = jnp.concatenate([leading, sample_field], axis=1)
    filtered = jnp.zeros(sample_field.shape, jnp.float32)
    for tap_index in range(TAPS):
        first_frame = TAPS - 1 - tap_index
        filtered = filtered + fir_taps[tap_index] * padded[:, first_frame:first_frame + FRAMES]
    spectrum = jnp.fft.rfft(filtered, axis=2)[:, :, :NCH]
    real_part = jnp.real(spectrum).astype(jnp.bfloat16)
    imag_part = jnp.imag(spectrum).astype(jnp.bfloat16)
    return jnp.stack([real_part, imag_part], axis=0)


def correlate(channel_data):
    stacked = jnp.concatenate([channel_data[0], channel_data[1]], axis=1)
    swapped = jnp.concatenate([channel_data[1], -channel_data[0]], axis=1)
    gram_re = jnp.dot(stacked, stacked.T, preferred_element_type=jnp.float32)
    gram_im = jnp.dot(swapped, stacked.T, preferred_element_type=jnp.float32)
    return jnp.stack([gram_re, gram_im], axis=0) / FRAMES


def reference(voltages, fir_taps):
    blocks = voltages.reshape(N_STN, INPUTS // N_STN, FRAMES, FRAME)
    spectra = lax.map(lambda input_block: channelise(input_block, fir_taps), blocks)
    by_channel = jnp.transpose(spectra, (4, 1, 0, 2, 3)).reshape(NCH, 2, INPUTS, FRAMES)
    return lax.map(correlate, by_channel)
```

```python
import functools

import jax
import jax.numpy as jnp
import numpy as np
from jax import lax
from jax.experimental import pallas as pl
from jax.experimental.pallas import tpu as pltpu
from jax.sharding import PartitionSpec as P

BF16 = jnp.bfloat16
F32 = jnp.float32
MESH = pl.DeviceIdType.MESH

TM, STN = 32, 8
ROWS = 128
FRAMES = 16
FRAME = 512
HALF = FRAME // 2
TAPS = 12
HALO = TAPS - 1
PAIRS = FRAMES // 2
ALL_INPUTS = ROWS * STN
ALL_FRAMES = FRAMES * TM
COLS = 256
COL_STEPS = ALL_INPUTS // COLS
HALO_PARTS = [(10, 1), (8, 2), (6, 2), (4, 2), (2, 2), (0, 2)]
STN_STEPS = [(1, 0), (3, 0), (0, 1), (1, 1), (3, 1), (2, 0), (2, 1)]


def dft_tables():
    index = np.arange(HALF)
    tables = []
    for parity in range(2):
        channel = 2 * np.arange(HALF // 2) + parity
        phase = (channel[:, None] * index[None, :]) % FRAME
        angle = phase * (2.0 * np.pi / FRAME)
        full = np.concatenate([np.cos(angle), -np.sin(angle)], axis=0)
        high = full.astype(BF16)
        low = (full - high.astype(np.float64)).astype(BF16)
        tables.append(np.stack([high, low]))
    return np.stack(tables)


def split(value):
    high = value.astype(BF16)
    return high, (value - high.astype(F32)).astype(BF16)


def nt_dot(left, right):
    return lax.dot_general(left, right, (((1,), (1,)), ((), ())), preferred_element_type=F32)


def correlator(
    volt_ref, taps_ref, table_ref, out_ref,
    x_buf, tap_buf, fold_buf, wide_buf, send_buf, spec_buf, left_buf, vis_buf,
    local_sem, halo_send_sem, halo_recv_sem, spec_sem, vis_sem,
):
    tm = lax.axis_index("tm")
    stn = lax.axis_index("stn")
    y_lo, z, core = tm // 16, (tm // 2) % 8, tm % 2
    x, y_hi = stn // 2, stn % 2

    own = pltpu.make_async_copy(
        volt_ref, x_buf.at[:, pl.ds(HALO * FRAME, FRAMES * FRAME)], local_sem.at[0]
    )
    own.start()

    def halo_copy(part):
        first, count = HALO_PARTS[part]
        return pltpu.make_async_remote_copy(
            src_ref=volt_ref.at[:, pl.ds((FRAMES - HALO + first) * FRAME, count * FRAME)],
            dst_ref=x_buf.at[:, pl.ds(first * FRAME, count * FRAME)],
            send_sem=halo_send_sem.at[part],
            recv_sem=halo_recv_sem.at[part],
            device_id=(tm + 1, stn),
            device_id_type=MESH,
        )

    @pl.when(tm < TM - 1)
    def _():
        for part in range(len(HALO_PARTS)):
            halo_copy(part).start()

    @pl.when(tm == 0)
    def _():
        x_buf[:, : HALO * FRAME] = jnp.zeros((ROWS, HALO * FRAME), BF16)

    for tap in range(TAPS):
        tap_buf[tap] = jnp.broadcast_to(taps_ref[tap : tap + 1, :], (16, FRAME))
    own.wait()

    def fir_pair(pair):
        base = pl.multiple_of(pair * 2 * FRAME, FRAME)

        def row_step(row_index, carry):
            row = pl.multiple_of(row_index * 16, 16)
            for lane in (0, 128):
                sums = []
                for part in range(2):
                    at = lane + part * HALF
                    totals = [None, None]
                    for frame in range(TAPS + 1):
                        value = x_buf[
                            pl.ds(row, 16), pl.ds(pl.multiple_of(base + frame * FRAME + at, 128), 128)
                        ].astype(F32)
                        for which in range(2):
                            tap = HALO + which - frame
                            if 0 <= tap < TAPS:
                                term = tap_buf[tap, :, at : at + 128] * value
                                totals[which] = term if totals[which] is None else totals[which] + term
                    sums.append(totals)
                for which in range(2):
                    even = sums[0][which] + sums[1][which]
                    odd = sums[0][which] - sums[1][which]
                    for parity, folded in enumerate((even, odd)):
                        high, low = split(folded)
                        at_row = pl.multiple_of(which * ROWS + row, 16)
                        fold_buf[parity, 0, pl.ds(at_row, 16), lane : lane + 128] = high
                        fold_buf[parity, 1, pl.ds(at_row, 16), lane : lane + 128] = low
            return carry

        lax.fori_loop(0, ROWS // 16, row_step, 0)

    def dft_pair(pair):
        for parity in range(2):
            high, low = fold_buf[parity, 0], fold_buf[parity, 1]
            result = (
                nt_dot(table_ref[parity, 0], high)
                + nt_dot(table_ref[parity, 1], high)
                + nt_dot(table_ref[parity, 0], low)
            )
            for which in range(2):
                for part in range(2):
                    first = (2 * parity + part) * FRAMES + 2 * pair + which
                    wide_buf[pl.ds(first, HALF // 2, stride=4 * FRAMES), :] = result[
                        part * 128 : (part + 1) * 128, which * ROWS : (which + 1) * ROWS
                    ]

    def pair_step(step, carry):
        pair = PAIRS - 1 - step
        for part in range(len(HALO_PARTS)):

            @pl.when((pair == len(HALO_PARTS) - 1 - part) & (tm > 0))
            def _():
                halo_copy(part).wait_recv()

        fir_pair(pair)
        dft_pair(pair)
        return carry

    lax.fori_loop(0, PAIRS, pair_step, 0)

    def pack_step(step, carry):
        rows = wide_buf[pl.ds(pl.multiple_of(step * 256, 256), 256), :]
        send_buf[pl.ds(step * 8, 8)] = rows.reshape(8, 2, FRAMES, ROWS).astype(BF16)
        return carry

    lax.fori_loop(0, HALF // 8, pack_step, 0)

    own_place = spec_buf.at[tm, :, :, pl.ds(pl.multiple_of(stn * ROWS, ROWS), ROWS)]
    keep = pltpu.make_async_copy(send_buf.at[tm * STN + stn], own_place, local_sem.at[1])
    keep.start()

    def send_step(step, carry):
        near = (step % 8) // 2
        d_z = jnp.where(step % 8 == 0, 4, jnp.where(step % 2 == 0, near, (8 - near) % 8))
        rest = step // 8
        to_core, rest = rest // 16, rest % 16
        to_x, rest = (x + rest % 4) % 4, rest // 4
        to_y_lo, to_y_hi = (y_lo + rest // 2) % 2, (y_hi + rest % 2) % 2
        to_tm = (to_y_lo * 8 + (z + d_z) % 8) * 2 + to_core
        to_stn = to_x * 2 + to_y_hi

        @pl.when((to_tm != tm) | (to_stn != stn))
        def _():
            pltpu.make_async_remote_copy(
                src_ref=send_buf.at[to_tm * STN + to_stn],
                dst_ref=own_place,
                send_sem=spec_sem.at[0],
                recv_sem=spec_sem.at[1],
                device_id=(to_tm, to_stn),
                device_id_type=MESH,
            ).start()

        return carry

    lax.fori_loop(0, TM * STN, send_step, 0)
    keep.wait()
    others = send_buf.at[pl.ds(0, TM * STN - 1)]
    pltpu.make_async_copy(others, others, spec_sem.at[1]).wait()

    def left_step(block, carry):
        at = pl.ds(pl.multiple_of(block * ROWS, ROWS), ROWS)
        real = spec_buf[:, 0, :, at].reshape(ALL_FRAMES, ROWS).T
        imag = spec_buf[:, 1, :, at].reshape(ALL_FRAMES, ROWS).T
        left_buf[block, 0, :, :ALL_FRAMES] = real
        left_buf[block, 0, :, ALL_FRAMES:] = imag
        left_buf[block, 1, :, :ALL_FRAMES] = imag
        left_buf[block, 1, :, ALL_FRAMES:] = -real
        return carry

    lax.fori_loop(0, STN, left_step, 0)

    def vis_copy(col_step, to_stn):
        at = pl.ds(pl.multiple_of(col_step * COLS, COLS), COLS)
        return vis_buf.at[col_step, to_stn], out_ref.at[stn, :, :, at]

    def col_loop(col_step, carry):
        at = pl.ds(pl.multiple_of(col_step * COLS, COLS), COLS)
        real = spec_buf[:, 0, :, at].reshape(ALL_FRAMES, COLS)
        imag = spec_buf[:, 1, :, at].reshape(ALL_FRAMES, COLS)

        def block_step(block, inner):
            left = left_buf[block].reshape(2 * ROWS, 2 * ALL_FRAMES)
            total = jnp.dot(left[:, :ALL_FRAMES], real, preferred_element_type=F32)
            total += jnp.dot(left[:, ALL_FRAMES:], imag, preferred_element_type=F32)
            vis_buf[col_step, block] = (total * (1.0 / ALL_FRAMES)).astype(BF16).reshape(2, ROWS, COLS)
            return inner

        lax.fori_loop(0, STN, block_step, 0)
        source, place = vis_copy(col_step, stn)
        pltpu.make_async_copy(source, place, local_sem.at[2]).start()
        for d_x, d_y in STN_STEPS:
            to_stn = ((x + d_x) % 4) * 2 + (y_hi + d_y) % 2
            source, place = vis_copy(col_step, to_stn)
            pltpu.make_async_remote_copy(
                src_ref=source,
                dst_ref=place,
                send_sem=vis_sem.at[0],
                recv_sem=vis_sem.at[1],
                device_id=(tm, to_stn),
                device_id_type=MESH,
            ).start()
        return carry

    lax.fori_loop(0, COL_STEPS, col_loop, 0)

    pltpu.make_async_copy(out_ref.at[0], out_ref.at[0], local_sem.at[2]).wait()
    pltpu.make_async_copy(others, others, spec_sem.at[0]).wait()
    received = out_ref.at[pl.ds(0, STN - 1)]
    pltpu.make_async_copy(received, received, vis_sem.at[0]).wait()
    pltpu.make_async_copy(received, received, vis_sem.at[1]).wait()

    @pl.when(tm < TM - 1)
    def _():
        for part in range(len(HALO_PARTS)):
            halo_copy(part).wait_send()


def per_device(voltages, fir_taps):
    tables = jnp.asarray(dft_tables())
    any_spec = pl.BlockSpec(memory_space=pl.ANY)
    vmem_spec = pl.BlockSpec(memory_space=pltpu.VMEM)
    vis = pl.pallas_call(
        correlator,
        out_shape=jax.ShapeDtypeStruct((STN, 2, ROWS, ALL_INPUTS), BF16),
        in_specs=[any_spec, vmem_spec, vmem_spec],
        out_specs=any_spec,
        scratch_shapes=[
            pltpu.VMEM((ROWS, (FRAMES + HALO) * FRAME), BF16),
            pltpu.VMEM((TAPS, 16, FRAME), F32),
            pltpu.VMEM((2, 2, 2 * ROWS, HALF), BF16),
            pltpu.VMEM((2 * HALF * FRAMES, ROWS), F32),
            pltpu.VMEM((HALF, 2, FRAMES, ROWS), BF16),
            pltpu.VMEM((TM, 2, FRAMES, ALL_INPUTS), BF16),
            pltpu.VMEM((STN, 2, ROWS, 2 * ALL_FRAMES), BF16),
            pltpu.VMEM((COL_STEPS, STN, 2, ROWS, COLS), BF16),
            pltpu.SemaphoreType.DMA((3,)),
            pltpu.SemaphoreType.DMA((len(HALO_PARTS),)),
            pltpu.SemaphoreType.DMA((len(HALO_PARTS),)),
            pltpu.SemaphoreType.DMA((2,)),
            pltpu.SemaphoreType.DMA((2,)),
        ],
        compiler_params=pltpu.CompilerParams(has_side_effects=True, vmem_limit_bytes=48 << 20),
        name="correlator",
    )(voltages, fir_taps, tables)
    return vis.astype(F32)


def solution(mesh):
    return jax.shard_map(
        per_device,
        mesh=mesh,
        in_specs=(P("stn", "tm"), P()),
        out_specs=P("tm", None, "stn", None),
        check_vma=False,
    )
```

```python
import functools

import jax
import jax.numpy as jnp
import numpy as np
from jax import lax
from jax.experimental import pallas as pl
from jax.experimental.pallas import tpu as pltpu
from jax.sharding import PartitionSpec as P

BF16 = jnp.bfloat16
F32 = jnp.float32
MESH = pl.DeviceIdType.MESH

TM, STN = 32, 8
ROWS = 128
FRAMES = 16
FRAME = 512
HALF = FRAME // 2
TAPS = 12
HALO = TAPS - 1
QUAD = 4
QUADS = FRAMES // QUAD
ALL_INPUTS = ROWS * STN
ALL_FRAMES = FRAMES * TM
SLOTS = HALF // 2
PLANES = SLOTS // 8
COLS = 256
COL_STEPS = ALL_INPUTS // COLS
BLOCKS = 4
AFTER = QUAD
BEFORE = HALO - AFTER
SPAN = BEFORE + FRAMES + AFTER
STN_STEPS = [(1, 0), (3, 0), (0, 1), (1, 1), (3, 1), (2, 0), (2, 1), (0, 0)]


def dft_tables():
    index = np.arange(HALF)
    tables = []
    for parity in range(2):
        y_lo, y_hi, x, z = np.indices((2, 2, 4, 8)).reshape(4, -1)
        channel = 16 * (8 * y_lo + z) + 8 * y_hi + 2 * x + parity
        phase = (channel[:, None] * index[None, :]) % FRAME
        angle = phase * (2.0 * np.pi / FRAME)
        full = np.concatenate([np.cos(angle), -np.sin(angle)], axis=0)
        high = full.astype(BF16)
        low = (full - high.astype(np.float64)).astype(BF16)
        tables.append(np.stack([high, low]))
    return np.stack(tables)


def split(value):
    high = value.astype(BF16)
    return high, (value - high.astype(F32)).astype(BF16)


def nt_dot(left, right):
    return lax.dot_general(left, right, (((1,), (1,)), ((), ())), preferred_element_type=F32)


def correlator(
    volt_ref, taps_ref, table_ref, out_ref,
    x_buf, tap_buf, fold_buf, wide_buf, send_buf, spec_buf, left_buf, vis_buf,
    local_sem, halo_send_sem, halo_recv_sem, spec_sem, vis_sem,
):
    tm = lax.axis_index("tm")
    stn = lax.axis_index("stn")
    y_lo, z, core = tm >> 4, (tm >> 1) & 7, tm & 1
    x, y_hi = stn >> 1, stn & 1

    own = pltpu.make_async_copy(
        volt_ref, x_buf.at[:, pl.ds(BEFORE * FRAME, FRAMES * FRAME)], local_sem.at[0]
    )
    own.start()

    barrier = pltpu.get_barrier_semaphore()

    def greet(step, carry):
        for to_stn in range(STN):

            def signal():
                pl.semaphore_signal(
                    barrier, inc=1, device_id=(tm ^ step, stn ^ to_stn), device_id_type=MESH
                )

            if to_stn:
                signal()
            else:
                pl.when(step > 0)(signal)
        return carry

    lax.fori_loop(0, TM, greet, 0)

    def halo_copy(part):
        source, place, count, to_tm = (
            (FRAMES - BEFORE, 0, QUAD, tm + 1),
            (FRAMES - BEFORE + QUAD, QUAD, BEFORE - QUAD, tm + 1),
            (0, BEFORE + FRAMES, AFTER, (tm - 1) & (TM - 1)),
        )[part]
        return pltpu.make_async_remote_copy(
            src_ref=volt_ref.at[:, pl.ds(source * FRAME, count * FRAME)],
            dst_ref=x_buf.at[:, pl.ds(place * FRAME, count * FRAME)],
            send_sem=halo_send_sem.at[part],
            recv_sem=halo_recv_sem.at[part],
            device_id=(to_tm, stn),
            device_id_type=MESH,
        )

    pl.semaphore_wait(barrier, TM * STN - 1)

    def start_before():
        @pl.when(tm < TM - 1)
        def _():
            halo_copy(1).start()
            halo_copy(0).start()

    @pl.when(core == 0)
    def _():
        start_before()
        halo_copy(2).start()

    @pl.when(core == 1)
    def _():
        halo_copy(2).start()
        start_before()

    for tap in range(TAPS):
        tap_buf[tap] = jnp.broadcast_to(taps_ref[tap : tap + 1, :], (16, FRAME))
    own.wait()

    def fir(quad):
        base = quad * QUAD * FRAME

        def row_step(row_index, carry):
            row = pl.multiple_of(row_index * 16, 16)
            for lane in (0, 128):
                sums = []
                for part in range(2):
                    at = lane + part * HALF
                    totals = [None] * QUAD
                    for frame in range(HALO + QUAD):
                        first = pl.multiple_of(base + frame * FRAME + at, 128)
                        value = x_buf[pl.ds(row, 16), pl.ds(first, 128)].astype(F32)
                        for which in range(QUAD):
                            tap = HALO + which - frame
                            if 0 <= tap < TAPS:
                                term = tap_buf[tap, :, at : at + 128] * value
                                totals[which] = term if totals[which] is None else totals[which] + term
                    sums.append(totals)
                for which in range(QUAD):
                    even = sums[0][which] + sums[1][which]
                    odd = sums[0][which] - sums[1][which]
                    rows = pl.ds(pl.multiple_of((quad * QUAD + which) * ROWS + row, 16), 16)
                    for parity, folded in enumerate((even, odd)):
                        high, low = split(folded)
                        fold_buf[parity, 0, rows, lane : lane + 128] = high
                        fold_buf[parity, 1, rows, lane : lane + 128] = low
            return carry

        lax.fori_loop(0, ROWS // 16, row_step, 0)

    def dft(quad, parity):
        rows = pl.ds(pl.multiple_of(quad * QUAD * ROWS, QUAD * ROWS), QUAD * ROWS)
        high, low = fold_buf[parity, 0, rows], fold_buf[parity, 1, rows]
        result = (
            nt_dot(table_ref[parity, 0], high)
            + nt_dot(table_ref[parity, 1], high)
            + nt_dot(table_ref[parity, 0], low)
        )
        for which in range(QUAD):
            for part in range(2):
                first = part * FRAMES + QUAD * quad + which
                wide_buf[parity, pl.ds(first, SLOTS, stride=2 * FRAMES), :] = result[
                    part * SLOTS : (part + 1) * SLOTS, which * ROWS : (which + 1) * ROWS
                ]

    quads = [2, jnp.where(core == 0, 3, 1), jnp.where(core == 0, 1, 0), jnp.where(core == 0, 0, 3)]
    @pl.when(tm == 0)
    def _():
        x_buf[:, : BEFORE * FRAME] = jnp.zeros((ROWS, BEFORE * FRAME), BF16)

    def wait_halo(quad):
        for part in range(2):

            @pl.when((quad == part) & (tm > 0))
            def _():
                halo_copy(part).wait_recv()

        @pl.when(quad == 3)
        def _():
            halo_copy(2).wait_recv()

        @pl.when((quad == 3) & (tm == TM - 1))
        def _():
            x_buf[:, 3 * QUAD * FRAME : (3 * QUAD + HALO) * FRAME] = jnp.zeros((ROWS, HALO * FRAME), BF16)

    for step in range(QUADS):
        if step > 0:
            wait_halo(quads[step])
        fir(quads[step])
        dft(quads[step], 0)
        if step < QUADS - 1:
            dft(quads[step], 1)

    own_place = spec_buf.at[tm, :, :, pl.ds(pl.multiple_of(stn * ROWS, ROWS), ROWS)]
    def send(parity):
        def plane_step(step, carry):
            to_x, to_y_hi, to_y_lo = x ^ (step & 3), y_hi ^ ((step >> 2) & 1), y_lo ^ (step >> 3)
            to_stn = to_x * 2 + to_y_hi
            plane = (to_y_lo * 2 + to_y_hi) * 4 + to_x
            rows = wide_buf[parity, pl.ds(pl.multiple_of(plane * 256, 256), 256), :]
            send_buf[parity, plane] = rows.reshape(8, 2, FRAMES, ROWS).astype(BF16)
            for d_z in (4, 1, 7, 2, 6, 3, 5, 0):
                to_z = (z + d_z) & 7
                source = send_buf.at[parity, plane, to_z]

                def start():
                    pltpu.make_async_remote_copy(
                        src_ref=source,
                        dst_ref=own_place,
                        send_sem=spec_sem.at[0],
                        recv_sem=spec_sem.at[1],
                        device_id=(to_y_lo * 16 + to_z * 2 + 1 - parity, to_stn),
                        device_id_type=MESH,
                    ).start()

                if d_z:
                    start()
                else:
                    pl.when((step > 0) | (core == parity))(start)

                    @pl.when((step == 0) & (core != parity))
                    def _():
                        pltpu.make_async_copy(source, own_place, spec_sem.at[1]).start()

            return carry

        lax.fori_loop(0, PLANES, plane_step, 0)

    send(0)
    dft(quads[-1], 1)
    send(1)

    everything = spec_buf.at[:, :, :, :]
    pltpu.make_async_copy(everything, everything, spec_sem.at[1]).wait()

    def left_step(block, carry):
        at = pl.ds(pl.multiple_of(block * ROWS, ROWS), ROWS)
        real = spec_buf[:, 0, :, at].reshape(ALL_FRAMES, ROWS).T
        imag = spec_buf[:, 1, :, at].reshape(ALL_FRAMES, ROWS).T
        left_buf[block, 0, :, :ALL_FRAMES] = real
        left_buf[block, 0, :, ALL_FRAMES:] = imag
        left_buf[block, 1, :, :ALL_FRAMES] = imag
        left_buf[block, 1, :, ALL_FRAMES:] = -real
        return carry

    lax.fori_loop(0, STN, left_step, 0)

    to_tm = (tm >> 1) * 2 + y_hi
    out_channel = x * 2 + 1 - core

    def col_loop(col_step, carry):
        at = pl.ds(pl.multiple_of(col_step * COLS, COLS), COLS)
        real = spec_buf[:, 0, :, at].reshape(ALL_FRAMES, COLS)
        imag = spec_buf[:, 1, :, at].reshape(ALL_FRAMES, COLS)

        def block_step(step, inner):
            blocks = pl.ds(step * BLOCKS, BLOCKS)
            left = left_buf[blocks].reshape(BLOCKS * 2 * ROWS, 2 * ALL_FRAMES)
            total = jnp.dot(left[:, :ALL_FRAMES], real, preferred_element_type=F32)
            total += jnp.dot(left[:, ALL_FRAMES:], imag, preferred_element_type=F32)
            total = (total * (1.0 / ALL_FRAMES)).astype(BF16)
            vis_buf[col_step, blocks] = total.reshape(BLOCKS, 2, ROWS, COLS)
            return inner

        lax.fori_loop(0, STN // BLOCKS, block_step, 0)
        place = out_ref.at[out_channel, :, :, at]
        for d_x, d_y in STN_STEPS:
            to_stn = ((x + d_x) & 3) * 2 + (y_hi ^ d_y)

            def start():
                pltpu.make_async_remote_copy(
                    src_ref=vis_buf.at[col_step, to_stn],
                    dst_ref=place,
                    send_sem=vis_sem.at[0],
                    recv_sem=vis_sem.at[1],
                    device_id=(to_tm, to_stn),
                    device_id_type=MESH,
                ).start()

            if d_x or d_y:
                start()
            else:
                pl.when(core != y_hi)(start)

        @pl.when(core == y_hi)
        def _():
            pltpu.make_async_copy(vis_buf.at[col_step, stn], place, vis_sem.at[1]).start()

        return carry

    lax.fori_loop(0, COL_STEPS, col_loop, 0)

    others = spec_buf.at[pl.ds(0, TM - 1)]
    pltpu.make_async_copy(others, others, spec_sem.at[0]).wait()
    rest = send_buf.at[0, 0, pl.ds(0, STN - 1)]
    pltpu.make_async_copy(rest, rest, spec_sem.at[0]).wait()
    sent = out_ref.at[pl.ds(0, STN - 1)]
    pltpu.make_async_copy(sent, sent, vis_sem.at[0]).wait()

    @pl.when(core != y_hi)
    def _():
        pltpu.make_async_copy(out_ref.at[0], out_ref.at[0], vis_sem.at[0]).wait()

    pltpu.make_async_copy(out_ref, out_ref, vis_sem.at[1]).wait()

    @pl.when(tm < TM - 1)
    def _():
        halo_copy(0).wait_send()
        halo_copy(1).wait_send()

    halo_copy(2).wait_send()


def per_device(voltages, fir_taps):
    tables = jnp.asarray(dft_tables())
    any_spec = pl.BlockSpec(memory_space=pl.ANY)
    vmem_spec = pl.BlockSpec(memory_space=pltpu.VMEM)
    vis = pl.pallas_call(
        correlator,
        out_shape=pltpu.VMEM((STN, 2, ROWS, ALL_INPUTS), BF16),
        in_specs=[any_spec, vmem_spec, vmem_spec],
        out_specs=any_spec,
        scratch_shapes=[
            pltpu.VMEM((ROWS, SPAN * FRAME), BF16),
            pltpu.VMEM((TAPS, 16, FRAME), F32),
            pltpu.VMEM((2, 2, FRAMES * ROWS, HALF), BF16),
            pltpu.VMEM((2, SLOTS * 2 * FRAMES, ROWS), F32),
            pltpu.VMEM((2, PLANES, 8, 2, FRAMES, ROWS), BF16),
            pltpu.VMEM((TM, 2, FRAMES, ALL_INPUTS), BF16),
            pltpu.VMEM((STN, 2, ROWS, 2 * ALL_FRAMES), BF16),
            pltpu.VMEM((COL_STEPS, STN, 2, ROWS, COLS), BF16),
            pltpu.SemaphoreType.DMA((1,)),
            pltpu.SemaphoreType.DMA((3,)),
            pltpu.SemaphoreType.DMA((3,)),
            pltpu.SemaphoreType.DMA((2,)),
            pltpu.SemaphoreType.DMA((2,)),
        ],
        compiler_params=pltpu.CompilerParams(
            collective_id=0, has_side_effects=True, vmem_limit_bytes=56 << 20
        ),
        name="correlator",
    )(voltages, fir_taps, tables)
    return vis.astype(F32)


def solution(mesh):
    return jax.shard_map(
        per_device,
        mesh=mesh,
        in_specs=(P("stn", "tm"), P()),
        out_specs=P("tm", None, "stn", None),
        check_vma=False,
    )
```

```python
import functools

import jax
import jax.numpy as jnp
import numpy as np
from jax import lax
from jax.experimental import pallas as pl
from jax.experimental.pallas import tpu as pltpu
from jax.sharding import PartitionSpec as P

BF16 = jnp.bfloat16
F32 = jnp.float32
MESH = pl.DeviceIdType.MESH

TM, STN = 32, 8
ROWS = 128
FRAMES = 16
FRAME = 512
HALF = FRAME // 2
TAPS = 12
HALO = TAPS - 1
QUAD = 4
QUADS = FRAMES // QUAD
ALL_INPUTS = ROWS * STN
ALL_FRAMES = FRAMES * TM
SLOTS = HALF // 2
PLANES = SLOTS // 8
COLS = 256
COL_STEPS = ALL_INPUTS // COLS
BLOCKS = 4
AFTER = QUAD
BEFORE = HALO - AFTER
SPAN = BEFORE + FRAMES + AFTER


def dft_tables():
    index = np.arange(HALF)
    tables = []
    for parity in range(2):
        y_lo, y_hi, x, z = np.indices((2, 2, 4, 8)).reshape(4, -1)
        channel = 16 * (8 * y_lo + z) + 8 * y_hi + 2 * x + parity
        phase = (channel[:, None] * index[None, :]) % FRAME
        angle = phase * (2.0 * np.pi / FRAME)
        full = np.concatenate([np.cos(angle), -np.sin(angle)], axis=0)
        high = full.astype(BF16)
        low = (full - high.astype(np.float64)).astype(BF16)
        tables.append(np.stack([high, low]))
    return np.stack(tables)


def split(value):
    high = value.astype(BF16)
    return high, (value - high.astype(F32)).astype(BF16)


def nt_dot(left, right):
    return lax.dot_general(left, right, (((1,), (1,)), ((), ())), preferred_element_type=F32)


def correlator(
    volt_ref, taps_any, table_any, out_ref,
    taps_ref, table_ref, x_buf, tap_buf, fold_buf, wide_buf, send_buf, spec_buf, left_buf, vis_buf,
    local_sem, halo_send_sem, halo_recv_sem, spec_sem, vis_sem,
):
    tm = lax.axis_index("tm")
    stn = lax.axis_index("stn")
    y_lo, z, core = tm >> 4, (tm >> 1) & 7, tm & 1
    x, y_hi = stn >> 1, stn & 1

    own = pltpu.make_async_copy(
        volt_ref, x_buf.at[:, pl.ds(BEFORE * FRAME, FRAMES * FRAME)], local_sem.at[0]
    )
    own.start()
    taps_copy = pltpu.make_async_copy(taps_any, taps_ref, local_sem.at[1])
    taps_copy.start()
    table_copy = pltpu.make_async_copy(table_any, table_ref, local_sem.at[2])
    table_copy.start()

    barrier = pltpu.get_barrier_semaphore()

    def greet(step, carry):
        for to_stn in range(STN):

            def signal():
                pl.semaphore_signal(
                    barrier, inc=1, device_id=(tm ^ step, stn ^ to_stn), device_id_type=MESH
                )

            if to_stn:
                signal()
            else:
                pl.when(step > 0)(signal)
        return carry

    lax.fori_loop(0, TM, greet, 0)

    def halo_copy(part):
        source, place, count, to_tm = (
            (FRAMES - BEFORE, 0, QUAD, tm + 1),
            (FRAMES - BEFORE + QUAD, QUAD, BEFORE - QUAD, tm + 1),
            (0, BEFORE + FRAMES, AFTER, (tm - 1) & (TM - 1)),
        )[part]
        return pltpu.make_async_remote_copy(
            src_ref=volt_ref.at[:, pl.ds(source * FRAME, count * FRAME)],
            dst_ref=x_buf.at[:, pl.ds(place * FRAME, count * FRAME)],
            send_sem=halo_send_sem.at[part],
            recv_sem=halo_recv_sem.at[part],
            device_id=(to_tm, stn),
            device_id_type=MESH,
        )

    pl.semaphore_wait(barrier, TM * STN - 1)

    def start_before():
        @pl.when(tm < TM - 1)
        def _():
            halo_copy(1).start()
            halo_copy(0).start()

    @pl.when(core == 0)
    def _():
        start_before()
        halo_copy(2).start()

    @pl.when(core == 1)
    def _():
        halo_copy(2).start()
        start_before()

    taps_copy.wait()
    for tap in range(TAPS):
        tap_buf[tap] = jnp.broadcast_to(taps_ref[tap : tap + 1, :], (16, FRAME))
    own.wait()
    table_copy.wait()

    def fir(quad):
        base = quad * QUAD * FRAME

        def row_step(row_index, carry):
            row = pl.multiple_of(row_index * 16, 16)
            for lane in (0, 128):
                sums = []
                for part in range(2):
                    at = lane + part * HALF
                    totals = [None] * QUAD
                    for frame in range(HALO + QUAD):
                        first = pl.multiple_of(base + frame * FRAME + at, 128)
                        value = x_buf[pl.ds(row, 16), pl.ds(first, 128)].astype(F32)
                        for which in range(QUAD):
                            tap = HALO + which - frame
                            if 0 <= tap < TAPS:
                                term = tap_buf[tap, :, at : at + 128] * value
                                totals[which] = term if totals[which] is None else totals[which] + term
                    sums.append(totals)
                for which in range(QUAD):
                    even = sums[0][which] + sums[1][which]
                    odd = sums[0][which] - sums[1][which]
                    rows = pl.ds(pl.multiple_of((quad * QUAD + which) * ROWS + row, 16), 16)
                    for parity, folded in enumerate((even, odd)):
                        high, low = split(folded)
                        fold_buf[parity, 0, rows, lane : lane + 128] = high
                        fold_buf[parity, 1, rows, lane : lane + 128] = low
            return carry

        lax.fori_loop(0, ROWS // 16, row_step, 0)

    def dft(quad, parity):
        rows = pl.ds(pl.multiple_of(quad * QUAD * ROWS, QUAD * ROWS), QUAD * ROWS)
        high, low = fold_buf[parity, 0, rows], fold_buf[parity, 1, rows]
        result = (
            nt_dot(table_ref[parity, 0], high)
            + nt_dot(table_ref[parity, 1], high)
            + nt_dot(table_ref[parity, 0], low)
        )
        for which in range(QUAD):
            for part in range(2):
                first = part * FRAMES + QUAD * quad + which
                wide_buf[parity, pl.ds(first, SLOTS, stride=2 * FRAMES), :] = result[
                    part * SLOTS : (part + 1) * SLOTS, which * ROWS : (which + 1) * ROWS
                ]

    quads = [2, jnp.where(core == 0, 3, 1), jnp.where(core == 0, 1, 0), jnp.where(core == 0, 0, 3)]
    @pl.when(tm == 0)
    def _():
        x_buf[:, : BEFORE * FRAME] = jnp.zeros((ROWS, BEFORE * FRAME), BF16)

    def wait_halo(quad):
        for part in range(2):

            @pl.when((quad == part) & (tm > 0))
            def _():
                halo_copy(part).wait_recv()

        @pl.when(quad == 3)
        def _():
            halo_copy(2).wait_recv()

        @pl.when((quad == 3) & (tm == TM - 1))
        def _():
            x_buf[:, 3 * QUAD * FRAME : (3 * QUAD + HALO) * FRAME] = jnp.zeros((ROWS, HALO * FRAME), BF16)

    for step in range(QUADS):
        if step > 0:
            wait_halo(quads[step])
        fir(quads[step])
        dft(quads[step], 0)
        if step < QUADS - 1:
            dft(quads[step], 1)

    own_place = spec_buf.at[tm, :, :, pl.ds(pl.multiple_of(stn * ROWS, ROWS), ROWS)]
    def send(parity):
        def plane_step(step, carry):
            to_x, to_y_hi, to_y_lo = x ^ (step & 3), y_hi ^ ((step >> 2) & 1), y_lo ^ (step >> 3)
            to_stn = to_x * 2 + to_y_hi
            plane = (to_y_lo * 2 + to_y_hi) * 4 + to_x
            rows = wide_buf[parity, pl.ds(pl.multiple_of(plane * 256, 256), 256), :]
            send_buf[parity, plane] = rows.reshape(8, 2, FRAMES, ROWS).astype(BF16)
            for d_z in (4, 1, 7, 2, 6, 3, 5, 0):
                to_z = (z + d_z) & 7
                source = send_buf.at[parity, plane, to_z]

                def start():
                    pltpu.make_async_remote_copy(
                        src_ref=source,
                        dst_ref=own_place,
                        send_sem=spec_sem.at[0],
                        recv_sem=spec_sem.at[1],
                        device_id=(to_y_lo * 16 + to_z * 2 + 1 - parity, to_stn),
                        device_id_type=MESH,
                    ).start()

                if d_z:
                    start()
                else:
                    pl.when((step > 0) | (core == parity))(start)

                    @pl.when((step == 0) & (core != parity))
                    def _():
                        pltpu.make_async_copy(source, own_place, spec_sem.at[1]).start()

            return carry

        lax.fori_loop(0, PLANES, plane_step, 0)

    send(0)
    dft(quads[-1], 1)
    send(1)

    everything = spec_buf.at[:, :, :, :]
    pltpu.make_async_copy(everything, everything, spec_sem.at[1]).wait()

    def left_step(block, carry):
        at = pl.ds(pl.multiple_of(block * ROWS, ROWS), ROWS)
        real = spec_buf[:, 0, :, at].reshape(ALL_FRAMES, ROWS).T
        imag = spec_buf[:, 1, :, at].reshape(ALL_FRAMES, ROWS).T
        left_buf[block, 0, :, :ALL_FRAMES] = real
        left_buf[block, 0, :, ALL_FRAMES:] = imag
        left_buf[block, 1, :, :ALL_FRAMES] = imag
        left_buf[block, 1, :, ALL_FRAMES:] = -real
        return carry

    to_tm = (tm >> 1) * 2 + y_hi
    out_channel = x * 2 + 1 - core

    def col_loop(col_step, carry):
        at = pl.ds(pl.multiple_of(col_step * COLS, COLS), COLS)
        real = spec_buf[:, 0, :, at].reshape(ALL_FRAMES, COLS)
        imag = spec_buf[:, 1, :, at].reshape(ALL_FRAMES, COLS)

        place = out_ref.at[out_channel, :, :, at]
        for half in range(2):
            first = ((stn >> 2) ^ 1 ^ half) * BLOCKS

            @pl.when(col_step == 0)
            def _():
                lax.fori_loop(0, BLOCKS, lambda step, carry: left_step(first + step, carry), 0)

            blocks = pl.ds(first, BLOCKS)
            left = left_buf[blocks].reshape(BLOCKS * 2 * ROWS, 2 * ALL_FRAMES)
            total = jnp.dot(left[:, :ALL_FRAMES], real, preferred_element_type=F32)
            total += jnp.dot(left[:, ALL_FRAMES:], imag, preferred_element_type=F32)
            total = (total * (1.0 / ALL_FRAMES)).astype(BF16)
            vis_buf[col_step, blocks] = total.reshape(BLOCKS, 2, ROWS, COLS)
            for low in (2, 1, 3, 0):
                to_stn = first + ((stn & 3) ^ low)

                def start():
                    pltpu.make_async_remote_copy(
                        src_ref=vis_buf.at[col_step, to_stn],
                        dst_ref=place,
                        send_sem=vis_sem.at[0],
                        recv_sem=vis_sem.at[1],
                        device_id=(to_tm, to_stn),
                        device_id_type=MESH,
                    ).start()

                if half == 0 or low:
                    start()
                else:
                    pl.when(core != y_hi)(start)

        @pl.when(core == y_hi)
        def _():
            pltpu.make_async_copy(vis_buf.at[col_step, stn], place, vis_sem.at[1]).start()

        return carry

    lax.fori_loop(0, COL_STEPS, col_loop, 0)

    others = spec_buf.at[pl.ds(0, TM - 1)]
    pltpu.make_async_copy(others, others, spec_sem.at[0]).wait()
    rest = send_buf.at[0, 0, pl.ds(0, STN - 1)]
    pltpu.make_async_copy(rest, rest, spec_sem.at[0]).wait()
    sent = out_ref.at[pl.ds(0, STN - 1)]
    pltpu.make_async_copy(sent, sent, vis_sem.at[0]).wait()

    @pl.when(core != y_hi)
    def _():
        pltpu.make_async_copy(out_ref.at[0], out_ref.at[0], vis_sem.at[0]).wait()

    pltpu.make_async_copy(out_ref, out_ref, vis_sem.at[1]).wait()

    @pl.when(tm < TM - 1)
    def _():
        halo_copy(0).wait_send()
        halo_copy(1).wait_send()

    halo_copy(2).wait_send()


def per_device(voltages, fir_taps):
    tables = jnp.asarray(dft_tables())
    any_spec = pl.BlockSpec(memory_space=pl.ANY)
    vis = pl.pallas_call(
        correlator,
        out_shape=pltpu.VMEM((STN, 2, ROWS, ALL_INPUTS), BF16),
        in_specs=[any_spec, any_spec, any_spec],
        out_specs=any_spec,
        scratch_shapes=[
            pltpu.VMEM((TAPS, FRAME), F32),
            pltpu.VMEM((2, 2, 2 * SLOTS, HALF), BF16),
            pltpu.VMEM((ROWS, SPAN * FRAME), BF16),
            pltpu.VMEM((TAPS, 16, FRAME), F32),
            pltpu.VMEM((2, 2, FRAMES * ROWS, HALF), BF16),
            pltpu.VMEM((2, SLOTS * 2 * FRAMES, ROWS), F32),
            pltpu.VMEM((2, PLANES, 8, 2, FRAMES, ROWS), BF16),
            pltpu.VMEM((TM, 2, FRAMES, ALL_INPUTS), BF16),
            pltpu.VMEM((STN, 2, ROWS, 2 * ALL_FRAMES), BF16),
            pltpu.VMEM((COL_STEPS, STN, 2, ROWS, COLS), BF16),
            pltpu.SemaphoreType.DMA((3,)),
            pltpu.SemaphoreType.DMA((3,)),
            pltpu.SemaphoreType.DMA((3,)),
            pltpu.SemaphoreType.DMA((2,)),
            pltpu.SemaphoreType.DMA((2,)),
        ],
        compiler_params=pltpu.CompilerParams(
            collective_id=0, has_side_effects=True, vmem_limit_bytes=56 << 20
        ),
        name="correlator",
    )(voltages, fir_taps, tables)
    return vis.astype(F32)


def solution(mesh):
    return jax.shard_map(
        per_device,
        mesh=mesh,
        in_specs=(P("stn", "tm"), P()),
        out_specs=P("tm", None, "stn", None),
        check_vma=False,
    )
```
